32 devices in a mesh: groups: 2 (over x), seq: 16 (over z, y, core).
Axes of the slice: x: 2, y: 2, z: 4, core: 2. Of those that a mesh axis runs over, the one named last changes fastest.
Arguments:
- inputs: bfloat16 [4, 8192, 768], P('groups', 'seq'), parts along dimension 0, may hold values from -6 to 6
- layer_norm_gain: float32 [768], replicated, may hold values from 0.1 to 1.9
- w_dilated: bfloat16 [3, 768, 384], replicated, may hold values from -0.125 to 0.125
- w_point: bfloat16 [384, 768], replicated, may hold values from -0.3125 to 0.3125
- cotangent: bfloat16 [4, 8192, 768], P('groups', 'seq'), parts along dimension 0, may hold values from -6 to 6
Outputs:
- outputs: bfloat16 [4, 8192, 768], P('groups', 'seq'), parts along dimension 0
- grad_inputs: bfloat16 [4, 8192, 768], P('groups', 'seq'), parts along dimension 0
- grad_dilated: float32 [6, 768, 384], P('groups', 'seq'), parts along dimension 0
- grad_point: float32 [768, 768], P('groups', 'seq'), parts along dimension 0
- grad_gain: float32 [1536], P(('groups', 'seq')), parts along dimension 0
The draws below stay inside these ranges and needn't reach their ends.
There are 2 independent parts, one for each index of `groups`. The reference program is written for one: setup_inputs(seed, part) draws one part's arguments, and reference() takes and returns one part's arrays. A program takes and returns all parts, laid end to end along the dimension named above; an argument that names none is the same for every part. Nothing has to cross between parts.
All inputs are finite; a program needn't handle non-finite values.
Results may differ from the reference program's by a relative error of at most 0.0053.
Values may be sent and summed in bfloat16 or wider, within the bound.
A program may use at most 128 MiB of HBM per device.

```python
import jax
import jax.numpy as jnp
from jax import lax

STREAM_CHANNELS = 768
NARROW_CHANNELS = 384
BATCH_SEQUENCES = 2
SEQUENCE_BINS = 8192
DILATION_BINS = 4096


def raised(result, key, source, target, shards_of, factor):
    owner, partner = [(jnp.arange(result.shape[position]) // (result.shape[position] // shards_of)).reshape([-1 if axis == position else 1 for axis in range(result.ndim)]) for position in (source, target)]
    chosen = jax.random.permutation(key, shards_of)[partner]
    strong = (owner == chosen) | (owner == (partner + shards_of // 2) % shards_of)
    return jnp.where(strong, factor * result, result)


def level_of(key, dims, cuts, least, high):
    factor_of, own = 1.0, jax.random.fold_in(key, 6)
    for axis_at, parts in cuts:
        steps = jnp.exp(jax.random.uniform(jax.random.fold_in(own, axis_at), (parts,), jnp.float32, least / len(cuts), high / len(cuts)))
        factor_of = factor_of * jnp.repeat(steps, dims[axis_at] // parts).reshape([-1 if axis == axis_at else 1 for axis in range(len(dims))])
    return factor_of


def bell_draw(own_key, shape, scale, bound, cuts=(), dtype=jnp.bfloat16):
    entries = scale * jax.random.normal(own_key, shape, jnp.float32)
    if cuts:
        entries = entries * level_of(own_key, shape, cuts, -0.22, 0.18)
    return jnp.clip(entries, -bound, bound).astype(dtype)


def gaussian_with(own_key, extent, deviation, most, pieces, heavy, kind=jnp.bfloat16):
    values = deviation * jax.random.normal(own_key, extent, jnp.float32)
    if pieces:
        values = values * level_of(own_key, extent, pieces, -0.22, 0.18)
    return jnp.clip(raised(values, jax.random.fold_in(own_key, 3), *heavy), -most, most).astype(kind)


def setup_inputs(seed: int = 0, part: int = 0) -> dict:
    keys = jax.random.split(jax.random.key(seed), 6)
    part_keys = jax.random.split(jax.random.fold_in(keys[5], part), 6)
    return {
        "inputs": gaussian_with(part_keys[0], (BATCH_SEQUENCES, SEQUENCE_BINS, STREAM_CHANNELS), 1.0, 6.0, ((1, 16),), (1, 2, 16, 2.0)),
        "layer_norm_gain": jnp.clip(1.0 + 0.18 * jax.random.normal(keys[1], (STREAM_CHANNELS,), jnp.float32), 0.1, 1.9),
        "w_dilated": bell_draw(keys[2], (3, STREAM_CHANNELS, NARROW_CHANNELS), (3 * STREAM_CHANNELS) ** -0.5, 0.125),
        "w_point": bell_draw(keys[3], (NARROW_CHANNELS, STREAM_CHANNELS), NARROW_CHANNELS ** -0.5, 0.3125),
        "cotangent": gaussian_with(part_keys[4], (BATCH_SEQUENCES, SEQUENCE_BINS, STREAM_CHANNELS), 1.0, 6.0, ((1, 16),), (1, 2, 16, 2.0)),
    }


def gelu_fn(value):
    return jax.nn.gelu(value, approximate=True)

def gelu_back(value, upstream):
    return jax.vjp(gelu_fn, value)[1](upstream)[0]

def reference(inputs, layer_norm_gain, w_dilated, w_point, cotangent):
    row_total_count = BATCH_SEQUENCES * SEQUENCE_BINS
    x_float = inputs.astype(jnp.float32)
    middle_offset = x_float - lax.optimization_barrier(jnp.mean(x_float, axis=-1, keepdims=True))
    inverse_deviation = lax.rsqrt(lax.optimization_barrier(jnp.mean(middle_offset * middle_offset, axis=-1, keepdims=True)) + 1e-05)
    standardized_input = middle_offset * inverse_deviation
    normalized_input = standardized_input * layer_norm_gain
    activated = gelu_fn(normalized_input).astype(jnp.bfloat16)
    padded_input = jnp.pad(activated, ((0, 0), (DILATION_BINS, DILATION_BINS), (0, 0)))
    kernel_taps = [padded_input[:, kernel_tap_index * DILATION_BINS:kernel_tap_index * DILATION_BINS + SEQUENCE_BINS].reshape(row_total_count, STREAM_CHANNELS) for kernel_tap_index in range(3)]
    pre = jnp.zeros((row_total_count, NARROW_CHANNELS), jnp.float32)
    for kernel_tap_index in range(3):
        pre = pre + jnp.dot(kernel_taps[kernel_tap_index], w_dilated[kernel_tap_index], preferred_element_type=jnp.float32)
    hid = gelu_fn(pre).astype(jnp.bfloat16)
    flat_in = x_float.reshape(row_total_count, STREAM_CHANNELS)
    outputs = (flat_in + jnp.dot(hid, w_point, preferred_element_type=jnp.float32)).astype(jnp.bfloat16)
    scale = lax.rsqrt(jnp.float32(row_total_count))
    grad_out = cotangent.reshape(row_total_count, STREAM_CHANNELS)
    grad_point = jnp.dot(hid.T, grad_out, preferred_element_type=jnp.float32) * scale
    grad_hid = jnp.dot(grad_out, w_point.T, preferred_element_type=jnp.float32)
    preactivation_gradient = gelu_back(pre, grad_hid).astype(jnp.bfloat16)
    grad_dilated = jnp.stack([jnp.dot(kernel_taps[kernel_tap_index].T, preactivation_gradient, preferred_element_type=jnp.float32) for kernel_tap_index in range(3)]) * scale
    padded_gradient = jnp.pad(preactivation_gradient.reshape(BATCH_SEQUENCES, SEQUENCE_BINS, NARROW_CHANNELS), ((0, 0), (DILATION_BINS, DILATION_BINS), (0, 0)))
    grad_act = jnp.zeros((row_total_count, STREAM_CHANNELS), jnp.float32)
    for kernel_tap_index in range(3):
        window_begin = (2 - kernel_tap_index) * DILATION_BINS
        piece = padded_gradient[:, window_begin:window_begin + SEQUENCE_BINS].reshape(row_total_count, NARROW_CHANNELS)
        grad_act = grad_act + jnp.dot(piece, w_dilated[kernel_tap_index].T, preferred_element_type=jnp.float32)
    flattened_standardized = standardized_input.reshape(row_total_count, STREAM_CHANNELS)
    normalized_gradient = gelu_back(normalized_input.reshape(row_total_count, STREAM_CHANNELS), grad_act)
    grad_gain = lax.optimization_barrier(jnp.sum(normalized_gradient * flattened_standardized, axis=0)) * scale
    input_gradient = normalized_gradient * layer_norm_gain
    flat_inv = inverse_deviation.reshape(row_total_count, 1)
    norm_part = flat_inv * (input_gradient - lax.optimization_barrier(jnp.mean(input_gradient, axis=-1, keepdims=True)) - flattened_standardized * lax.optimization_barrier(jnp.mean(input_gradient * flattened_standardized, axis=-1, keepdims=True)))
    grad_inputs = (grad_out.astype(jnp.float32) + norm_part).astype(jnp.bfloat16)
    return (outputs.reshape(BATCH_SEQUENCES, SEQUENCE_BINS, STREAM_CHANNELS), grad_inputs.reshape(BATCH_SEQUENCES, SEQUENCE_BINS, STREAM_CHANNELS), grad_dilated, grad_point, grad_gain)
```

```python
import jax
import jax.numpy as jnp
from jax import lax
from jax.sharding import PartitionSpec as P

DILATION = 4096
F32, BF16 = jnp.float32, jnp.bfloat16


def gelu_fn(value):
    return jax.nn.gelu(value, approximate=True)


def gelu_back(value, upstream):
    return jax.vjp(gelu_fn, value)[1](upstream)[0]


def dot(a, b):
    return jnp.dot(a, b, preferred_element_type=F32)


def dot_rows(a, b):
    return lax.dot_general(a, b, (((0,), (0,)), ((), ())), preferred_element_type=F32)


def dot_last(a, b):
    return lax.dot_general(a, b, (((1,), (1,)), ((), ())), preferred_element_type=F32)


def swap(value, bit):
    n = lax.axis_size("seq")
    return lax.ppermute(value, "seq", [(s, s ^ bit) for s in range(n)])


def shifted(value, steps):
    n = lax.axis_size("seq")
    return lax.ppermute(
        value, "seq", [(s, s + steps) for s in range(max(0, -steps), min(n, n - steps))]
    )


def halves(blocks, bit):
    pairs = blocks.reshape(blocks.shape[0] // 2, 2, *blocks.shape[1:])
    mine = (lax.axis_index("seq") & bit) != 0
    keep = jnp.where(mine, pairs[:, 1], pairs[:, 0])
    send = jnp.where(mine, pairs[:, 0], pairs[:, 1])
    return keep, send.astype(BF16)


def reduced(blocks, last=True):
    n = lax.axis_size("seq")
    bit = 1
    while bit < (n if last else n // 2):
        keep, send = halves(blocks, bit)
        blocks = keep + swap(send, bit).astype(F32)
        bit *= 2
    return blocks


def per_device(inputs, gain, w_dilated, w_point, cotangent):
    num_seqs, bins, channels = inputs.shape
    narrow = w_point.shape[0]
    n = lax.axis_size("seq")
    hops = DILATION // bins
    paired = n == 2 * hops
    rows_total = num_seqs * bins * n
    scale = lax.rsqrt(F32(rows_total))
    shard = channels // n
    upper = lax.axis_index("seq") >= hops

    if paired:
        w_far = jnp.where(upper, w_dilated[2], w_dilated[0])
        w_all = jnp.concatenate([w_far, w_dilated[1]], axis=1)
    else:
        w_all = jnp.concatenate([w_dilated[0], w_dilated[2], w_dilated[1]], axis=1)

    def exchange(value):
        if paired:
            return [swap(value[0], hops)]
        return [shifted(value[0], hops), shifted(value[-1], -hops)]

    def normalize(b):
        x = inputs[b].astype(F32)
        mid = x - jnp.mean(x, axis=-1, keepdims=True)
        inv = lax.rsqrt(jnp.mean(mid * mid, axis=-1, keepdims=True) + 1e-05)
        return x, mid * inv, inv

    acts, own, sent = [], [], []
    for b in range(num_seqs):
        _, xhat, _ = normalize(b)
        act = gelu_fn(xhat * gain).astype(BF16)
        acts.append(act)
        product = dot(act, w_all)
        far = product[:, :-narrow].astype(BF16)
        own.append(product[:, -narrow:])
        sent.append(exchange([far[:, :narrow], far[:, -narrow:]]))

    outs, hids, grads_pre, arrived = [], [], [], []
    for b in range(num_seqs):
        grad_hid = dot_last(cotangent[b], w_point)
        pre = own[b]
        for term in sent[b]:
            pre = pre + term.astype(F32)
        hid = gelu_fn(pre).astype(BF16)
        grad_pre = gelu_back(pre, grad_hid).astype(BF16)
        arrived.append(exchange([grad_pre, grad_pre]))
        hids.append(hid)
        grads_pre.append(grad_pre)
        outs.append((inputs[b].astype(F32) + dot(hid, w_point)).astype(BF16))
    outputs = jnp.stack(outs)

    act_all = jnp.concatenate(acts)
    point_terms = dot_rows(cotangent.reshape(-1, channels), jnp.concatenate(hids))
    centre_terms = dot_rows(act_all, jnp.concatenate(grads_pre))
    early = jnp.concatenate(
        [centre_terms.reshape(n, shard, narrow), point_terms.reshape(n, shard, narrow)], axis=1
    )
    early = reduced(early)[0] * scale

    grad_in, gain_terms = [], jnp.zeros((channels,), F32)
    for b in range(num_seqs):
        _, xhat, inv = normalize(b)
        normed = xhat * gain
        if paired:
            back = jnp.concatenate([arrived[b][0], grads_pre[b]], axis=1)
        else:
            back = jnp.concatenate([arrived[b][1], arrived[b][0], grads_pre[b]], axis=1)
        grad_act = dot_last(back, w_all)
        grad_normed = gelu_back(normed, grad_act)
        gain_terms = gain_terms + jnp.sum(grad_normed * xhat, axis=0)
        gx = grad_normed * gain
        part = inv * (
            gx
            - jnp.mean(gx, axis=-1, keepdims=True)
            - xhat * jnp.mean(gx * xhat, axis=-1, keepdims=True)
        )
        grad_in.append((cotangent[b].astype(F32) + part).astype(BF16))
    grad_inputs = jnp.stack(grad_in)

    gain_block = jnp.pad(gain_terms.reshape(n, 1, shard), ((0, 0), (0, 15), (0, narrow - shard)))
    if paired:
        far_terms = dot_rows(act_all, jnp.concatenate([a[0] for a in arrived]))
        late = jnp.concatenate([far_terms.reshape(n, shard, narrow), gain_block], axis=1)
        late = reduced(late, last=False)
        keep, send = halves(late, n // 2)
        keep, other = keep[0], swap(send, n // 2)[0].astype(F32)
        first = jnp.where(upper, other[:shard], keep[:shard])
        final = jnp.where(upper, keep[:shard], other[:shard])
        gain_sum = keep[shard, :shard] + other[shard, :shard]
    else:
        zero_terms = dot_rows(act_all, jnp.concatenate([a[1] for a in arrived]))
        two_terms = dot_rows(act_all, jnp.concatenate([a[0] for a in arrived]))
        late = jnp.concatenate(
            [zero_terms.reshape(n, shard, narrow), two_terms.reshape(n, shard, narrow), gain_block],
            axis=1,
        )
        late = reduced(late)[0]
        first, final = late[:shard], late[shard : 2 * shard]
        gain_sum = late[2 * shard, :shard]
    grad_dilated = jnp.stack([first * scale, early[:shard], final * scale])
    return outputs, grad_inputs, grad_dilated, early[shard:].T, gain_sum * scale


def solution(mesh):
    in_specs = (P("groups", "seq", None), P(), P(), P(), P("groups", "seq", None))
    out_specs = (
        P("groups", "seq", None),
        P("groups", "seq", None),
        P("groups", "seq", None),
        P("groups", "seq"),
        P(("groups", "seq")),
    )
    return jax.shard_map(
        per_device, mesh=mesh, in_specs=in_specs, out_specs=out_specs, check_vma=False
    )
```

```python
import jax
import jax.numpy as jnp
from jax import lax
from jax.sharding import PartitionSpec as P

DILATION = 4096
F32, BF16 = jnp.float32, jnp.bfloat16


def gelu_fn(value):
    return jax.nn.gelu(value, approximate=True)


def gelu_back(value, upstream):
    return jax.vjp(gelu_fn, value)[1](upstream)[0]


def dot(a, b):
    return jnp.dot(a, b, preferred_element_type=F32)


def dot_rows(a, b):
    return lax.dot_general(a, b, (((0,), (0,)), ((), ())), preferred_element_type=F32)


def dot_last(a, b):
    return lax.dot_general(a, b, (((1,), (1,)), ((), ())), preferred_element_type=F32)


def swap(value, bit):
    n = lax.axis_size("seq")
    return lax.ppermute(value, "seq", [(s, s ^ bit) for s in range(n)])


def shifted(value, steps):
    n = lax.axis_size("seq")
    return lax.ppermute(
        value, "seq", [(s, s + steps) for s in range(max(0, -steps), min(n, n - steps))]
    )


def halves(blocks, bit):
    pairs = blocks.reshape(blocks.shape[0] // 2, 2, *blocks.shape[1:])
    mine = (lax.axis_index("seq") & bit) != 0
    keep = jnp.where(mine, pairs[:, 1], pairs[:, 0])
    send = jnp.where(mine, pairs[:, 0], pairs[:, 1])
    return keep, send.astype(BF16)


def reduced(blocks, last=True):
    n = lax.axis_size("seq")
    bit = 1
    while bit < (n if last else n // 2):
        keep, send = halves(blocks, bit)
        blocks = keep + swap(send, bit).astype(F32)
        bit *= 2
    return blocks


def per_device(inputs, gain, w_dilated, w_point, cotangent):
    num_seqs, bins, channels = inputs.shape
    narrow = w_point.shape[0]
    n = lax.axis_size("seq")
    hops = DILATION // bins
    paired = n == 2 * hops
    rows_total = num_seqs * bins * n
    scale = lax.rsqrt(F32(rows_total))
    shard = channels // n
    upper = lax.axis_index("seq") >= hops

    if paired:
        w_far = lax.dynamic_index_in_dim(w_dilated, jnp.where(upper, 2, 0), 0, keepdims=False)
    else:
        w_far = jnp.concatenate([w_dilated[0], w_dilated[2]], axis=1)
    w_all = jnp.concatenate([w_far, w_dilated[1]], axis=1)

    def exchange(value):
        if paired:
            return [swap(value[0], hops)]
        return [shifted(value[0], hops), shifted(value[-1], -hops)]

    def normalize(b):
        x = inputs[b].astype(F32)
        mid = x - jnp.mean(x, axis=-1, keepdims=True)
        inv = lax.rsqrt(jnp.mean(mid * mid, axis=-1, keepdims=True) + 1e-05)
        return x, mid * inv, inv

    acts, own, sent = [], [], []
    for b in range(num_seqs):
        _, xhat, _ = normalize(b)
        act = gelu_fn(xhat * gain).astype(BF16)
        acts.append(act)
        far = dot(act, w_far).astype(BF16)
        own.append(dot(act, w_dilated[1]))
        sent.append(exchange([far[:, :narrow], far[:, -narrow:]]))

    outs, hids, grads_pre, arrived = [], [], [], []
    for b in range(num_seqs):
        grad_hid = dot_last(cotangent[b], w_point)
        pre = own[b]
        for term in sent[b]:
            pre = pre + term.astype(F32)
        hid = gelu_fn(pre).astype(BF16)
        grad_pre = gelu_back(pre, grad_hid).astype(BF16)
        arrived.append(exchange([grad_pre, grad_pre]))
        hids.append(hid)
        grads_pre.append(grad_pre)
        outs.append((inputs[b].astype(F32) + dot(hid, w_point)).astype(BF16))
    outputs = jnp.stack(outs)

    act_all = jnp.concatenate(acts)
    point_terms = dot_rows(cotangent.reshape(-1, channels), jnp.concatenate(hids))
    centre_terms = dot_rows(act_all, jnp.concatenate(grads_pre))
    early = jnp.concatenate(
        [centre_terms.reshape(n, shard, narrow), point_terms.reshape(n, shard, narrow)], axis=1
    )
    early = reduced(early, last=False)
    arrived, early = lax.optimization_barrier((arrived, early))
    if paired:
        far_terms = dot_rows(act_all, jnp.concatenate([a[0] for a in arrived]))
        late = reduced(far_terms.reshape(n, shard, narrow), last=False)
    else:
        zero_terms = dot_rows(act_all, jnp.concatenate([a[1] for a in arrived]))
        two_terms = dot_rows(act_all, jnp.concatenate([a[0] for a in arrived]))
        late = reduced(
            jnp.concatenate(
                [zero_terms.reshape(n, shard, narrow), two_terms.reshape(n, shard, narrow)], axis=1
            ),
            last=False,
        )
    keep, send = halves(jnp.concatenate([early, late], axis=1), n // 2)
    keep, other = keep[0], swap(send, n // 2)[0].astype(F32)
    early = (keep[: 2 * shard] + other[: 2 * shard]) * scale
    keep, other = keep[2 * shard :], other[2 * shard :]
    if paired:
        first, final = jnp.where(upper, other, keep), jnp.where(upper, keep, other)
    else:
        first, final = keep[:shard] + other[:shard], keep[shard:] + other[shard:]

    grad_in, gain_terms = [], jnp.zeros((channels,), F32)
    for b in range(num_seqs):
        _, xhat, inv = normalize(b)
        normed = xhat * gain
        if paired:
            back = jnp.concatenate([arrived[b][0], grads_pre[b]], axis=1)
        else:
            back = jnp.concatenate([arrived[b][1], arrived[b][0], grads_pre[b]], axis=1)
        grad_act = dot_last(back, w_all)
        grad_normed = gelu_back(normed, grad_act)
        gain_terms = gain_terms + jnp.sum(grad_normed * xhat, axis=0)
        gx = grad_normed * gain
        part = inv * (
            gx
            - jnp.mean(gx, axis=-1, keepdims=True)
            - xhat * jnp.mean(gx * xhat, axis=-1, keepdims=True)
        )
        grad_in.append((cotangent[b].astype(F32) + part).astype(BF16))
    grad_inputs = jnp.stack(grad_in)

    gain_sum = reduced(gain_terms.reshape(n, 1, shard))[0, 0]
    grad_dilated = jnp.stack([first * scale, early[:shard], final * scale])
    return outputs, grad_inputs, grad_dilated, early[shard:].T, gain_sum * scale


def solution(mesh):
    in_specs = (P("groups", "seq", None), P(), P(), P(), P("groups", "seq", None))
    out_specs = (
        P("groups", "seq", None),
        P("groups", "seq", None),
        P("groups", "seq", None),
        P("groups", "seq"),
        P(("groups", "seq")),
    )
    return jax.shard_map(
        per_device, mesh=mesh, in_specs=in_specs, out_specs=out_specs, check_vma=False
    )
```

```python
import jax
import jax.numpy as jnp
from jax import lax
from jax.experimental import pallas as pl
from jax.experimental.pallas import tpu as pltpu
from jax.sharding import PartitionSpec as P

DILATION = 4096
F32, BF16 = jnp.float32, jnp.bfloat16


def gelu_fn(value):
    return jax.nn.gelu(value, approximate=True)


def gelu_back(value, upstream):
    return jax.vjp(gelu_fn, value)[1](upstream)[0]


def dot(a, b):
    return jnp.dot(a, b, preferred_element_type=F32)


def dot_rows(a, b):
    return lax.dot_general(a, b, (((0,), (0,)), ((), ())), preferred_element_type=F32)


def dot_last(a, b):
    return lax.dot_general(a, b, (((1,), (1,)), ((), ())), preferred_element_type=F32)


def swap(value, bit):
    n = lax.axis_size("seq")
    return lax.ppermute(value, "seq", [(s, s ^ bit) for s in range(n)])


def shifted(value, steps):
    n = lax.axis_size("seq")
    return lax.ppermute(
        value, "seq", [(s, s + steps) for s in range(max(0, -steps), min(n, n - steps))]
    )


def halves(blocks, bit):
    pairs = blocks.reshape(blocks.shape[0] // 2, 2, *blocks.shape[1:])
    mine = (lax.axis_index("seq") & bit) != 0
    keep = jnp.where(mine, pairs[:, 1], pairs[:, 0])
    send = jnp.where(mine, pairs[:, 0], pairs[:, 1])
    return keep, send.astype(BF16)


def reduced(blocks, last=True):
    n = lax.axis_size("seq")
    bit = 1
    while bit < (n if last else n // 2):
        keep, send = halves(blocks, bit)
        blocks = keep + swap(send, bit).astype(F32)
        bit *= 2
    return blocks


def per_device(inputs, gain, w_dilated, w_point, cotangent):
    num_seqs, bins, channels = inputs.shape
    narrow = w_point.shape[0]
    n = lax.axis_size("seq")
    hops = DILATION // bins
    paired = n == 2 * hops
    rows_total = num_seqs * bins * n
    scale = lax.rsqrt(F32(rows_total))
    shard = channels // n
    upper = lax.axis_index("seq") >= hops

    if paired:
        w_far = jnp.where(upper, w_dilated[2], w_dilated[0])
        w_all = jnp.concatenate([w_far, w_dilated[1]], axis=1)
    else:
        w_all = jnp.concatenate([w_dilated[0], w_dilated[2], w_dilated[1]], axis=1)

    def exchange(value):
        if paired:
            return [swap(value[0], hops)]
        return [shifted(value[0], hops), shifted(value[-1], -hops)]

    def normalize(b):
        x = inputs[b].astype(F32)
        mid = x - jnp.mean(x, axis=-1, keepdims=True)
        inv = lax.rsqrt(jnp.mean(mid * mid, axis=-1, keepdims=True) + 1e-05)
        return x, mid * inv, inv

    acts, own, sent = [], [], []
    for b in range(num_seqs):
        _, xhat, _ = normalize(b)
        act = gelu_fn(xhat * gain).astype(BF16)
        acts.append(act)
        product = dot(act, w_all)
        far = product[:, :-narrow].astype(BF16)
        own.append(product[:, -narrow:])
        sent.append(exchange([far[:, :narrow], far[:, -narrow:]]))

    outs, hids, grads_pre, arrived = [], [], [], []
    for b in range(num_seqs):
        grad_hid = dot_last(cotangent[b], w_point)
        pre = own[b]
        for term in sent[b]:
            pre = pre + term.astype(F32)
        hid = gelu_fn(pre).astype(BF16)
        grad_pre = gelu_back(pre, grad_hid).astype(BF16)
        arrived.append(exchange([grad_pre, grad_pre]))
        hids.append(hid)
        grads_pre.append(grad_pre)
        outs.append((inputs[b].astype(F32) + dot(hid, w_point)).astype(BF16))
    outputs = jnp.stack(outs)

    act_all = jnp.concatenate(acts)
    point_terms = dot_rows(cotangent.reshape(-1, channels), jnp.concatenate(hids))
    centre_terms = dot_rows(act_all, jnp.concatenate(grads_pre))
    early = jnp.concatenate(
        [centre_terms.reshape(n, shard, narrow), point_terms.reshape(n, shard, narrow)], axis=1
    )
    early = reduced(early)[0] * scale

    grad_in, gain_terms = [], jnp.zeros((channels,), F32)
    for b in range(num_seqs):
        _, xhat, inv = normalize(b)
        normed = xhat * gain
        if paired:
            back = jnp.concatenate([arrived[b][0], grads_pre[b]], axis=1)
        else:
            back = jnp.concatenate([arrived[b][1], arrived[b][0], grads_pre[b]], axis=1)
        grad_act = dot_last(back, w_all)
        grad_normed = gelu_back(normed, grad_act)
        gain_terms = gain_terms + jnp.sum(grad_normed * xhat, axis=0)
        gx = grad_normed * gain
        part = inv * (
            gx
            - jnp.mean(gx, axis=-1, keepdims=True)
            - xhat * jnp.mean(gx * xhat, axis=-1, keepdims=True)
        )
        grad_in.append((cotangent[b].astype(F32) + part).astype(BF16))
    grad_inputs = jnp.stack(grad_in)

    gain_block = jnp.pad(gain_terms.reshape(n, 1, shard), ((0, 0), (0, 15), (0, narrow - shard)))
    if paired:
        far_terms = dot_rows(act_all, jnp.concatenate([a[0] for a in arrived]))
        late = jnp.concatenate([far_terms.reshape(n, shard, narrow), gain_block], axis=1)
        late = reduced(late, last=False)
        keep, send = halves(late, n // 2)
        keep, other = keep[0], swap(send, n // 2)[0].astype(F32)
        first = jnp.where(upper, other[:shard], keep[:shard])
        final = jnp.where(upper, keep[:shard], other[:shard])
        gain_sum = keep[shard, :shard] + other[shard, :shard]
    else:
        zero_terms = dot_rows(act_all, jnp.concatenate([a[1] for a in arrived]))
        two_terms = dot_rows(act_all, jnp.concatenate([a[0] for a in arrived]))
        late = jnp.concatenate(
            [zero_terms.reshape(n, shard, narrow), two_terms.reshape(n, shard, narrow), gain_block],
            axis=1,
        )
        late = reduced(late)[0]
        first, final = late[:shard], late[shard : 2 * shard]
        gain_sum = late[2 * shard, :shard]
    grad_dilated = jnp.stack([first * scale, early[:shard], final * scale])
    return outputs, grad_inputs, grad_dilated, early[shard:].T, gain_sum * scale

CHUNKS = 4
ROOT = 0.7978845608028654


def gelu_parts(v):
    square = v * v
    t = jnp.tanh(ROOT * v * (1.0 + 0.044715 * square))
    half = 0.5 * (1.0 + t)
    slope = half + 0.5 * v * (1.0 - t * t) * (ROOT * (1.0 + 3 * 0.044715 * square))
    return v * half, slope


def block_kernel(
    n, x_ref, gain_ref, w_ref, wp_ref, cot_ref,
    out_ref, gin_ref, gd_ref, gp_ref, gg_ref,
    act, own, p_send, p_recv, q, q_recv, hid, slope, mean_s, inv_s,
    early, late, gain_acc, e_send, e_recv, l_send, l_recv, g_send, g_recv,
    p_sems, q_sems, e_sems, l_sems, g_sems,
):
    me = lax.axis_index("seq")
    rows, channels = x_ref.shape
    narrow = wp_ref.shape[0]
    shard = channels // n
    size = rows // CHUNKS
    bits, bit = [], 1
    while bit < n:
        bits.append(bit)
        bit *= 2
    mine = [(me // b) % 2 for b in bits]
    partners = [me + b * (1 - 2 * m) for b, m in zip(bits, mine)]
    upper = mine[-1]
    far_tap = 2 * upper
    scale = F32((rows * n) ** -0.5)

    barrier = pltpu.get_barrier_semaphore()
    for partner in partners:
        pl.semaphore_signal(
            barrier, inc=1, device_id={"seq": partner}, device_id_type=pl.DeviceIdType.MESH
        )

    def remote(src, dst, sems, i, level):
        return pltpu.make_async_remote_copy(
            src_ref=src, dst_ref=dst, send_sem=sems.at[0, i], recv_sem=sems.at[1, i],
            device_id={"seq": partners[level]}, device_id_type=pl.DeviceIdType.MESH,
        )

    def span(c):
        return pl.ds(pl.multiple_of(c * size, size), size)

    def p_copy(c):
        return remote(p_send.at[span(c)], p_recv.at[span(c)], p_sems, c, -1)

    def q_copy(c):
        return remote(q.at[span(c)], q_recv.at[span(c)], q_sems, c, -1)

    def first_part(c):
        r = span(c)
        x = x_ref[r, :].astype(F32)
        mean = jnp.mean(x, axis=-1, keepdims=True)
        mid = x - mean
        inv = lax.rsqrt(jnp.mean(mid * mid, axis=-1, keepdims=True) + 1e-05)
        value, grad = gelu_parts(mid * inv * gain_ref[...])
        value = value.astype(BF16)
        p_send[r, :] = dot(value, w_ref[far_tap]).astype(BF16)
        act[r, :] = value
        slope[r, :] = grad
        mean_s[r, :] = mean
        inv_s[r, :] = inv

    first_part(0)
    pl.semaphore_wait(barrier, len(bits))
    p_copy(0).start()

    @pl.loop(1, CHUNKS)
    def _(c):
        first_part(c)
        p_copy(c).start()

    @pl.loop(0, CHUNKS)
    def _(c):
        r = span(c)
        own[r, :] = dot(act[r, :], w_ref[1])

    @pl.loop(0, CHUNKS)
    def _(c):
        r = span(c)
        grad_hid = dot_last(cot_ref[r, :], wp_ref[...])
        p_copy(c).wait_recv()
        value, grad = gelu_parts(own[r, :] + p_recv[r, :].astype(F32))
        q[r, :] = (grad * grad_hid).astype(BF16)
        q_copy(c).start()
        value = value.astype(BF16)
        hid[r, :] = value
        out_ref[r, :] = (x_ref[r, :].astype(F32) + dot(value, wp_ref[...])).astype(BF16)

    cut = n // 2
    for j in range(2):
        cols = slice(j * cut * shard, (j + 1) * cut * shard)
        part = slice(j * cut, (j + 1) * cut)
        early[part, :shard, :] = dot_rows(act[:, cols], q[...]).reshape(cut, shard, narrow)
        early[part, shard:, :] = dot_rows(cot_ref[:, cols], hid[...]).reshape(cut, shard, narrow)

    def send_half(level, cur, sends, recvs, sems):
        count = n >> (level + 1)
        base = n - 2 * count

        @pl.loop(0, count)
        def _(i):
            sends[base + i] = cur[2 * i + 1 - mine[level]].astype(BF16)

        copy = remote(
            sends.at[pl.ds(base, count)], recvs.at[pl.ds(base, count)], sems, level, level
        )
        copy.start()
        return copy

    def add_half(level, cur, recvs, copy):
        count = n >> (level + 1)
        base = n - 2 * count
        copy.wait_recv()

        @pl.loop(0, count)
        def _(i):
            cur[i] = cur[2 * i + mine[level]] + recvs[base + i].astype(F32)

    waits = []
    last = len(bits) - 1

    def back_part(c):
        r = span(c)
        grad_act = dot_last(q[r, :], w_ref[1]) + dot_last(q_recv[r, :], w_ref[far_tap])
        inv = inv_s[r, :]
        xhat = (x_ref[r, :].astype(F32) - mean_s[r, :]) * inv
        gn = grad_act * slope[r, :]
        gain_acc[...] += jnp.sum((gn * xhat).reshape(size // 8, 8, channels), axis=0)
        gx = gn * gain_ref[...]
        m1 = jnp.mean(gx, axis=-1, keepdims=True)
        m2 = jnp.mean(gx * xhat, axis=-1, keepdims=True)
        gin_ref[r, :] = (cot_ref[r, :].astype(F32) + inv * (gx - m1 - xhat * m2)).astype(BF16)

    gain_acc[...] = jnp.zeros_like(gain_acc)
    for level in range(last):
        copy = send_half(level, early, e_send, e_recv, e_sems)
        waits.append(copy)
        q_copy(level).wait_recv()
        if level < CHUNKS - 1:
            back_part(level)
        add_half(level, early, e_recv, copy)
    e_last = send_half(last, early, e_send, e_recv, e_sems)
    waits.append(e_last)
    head = (CHUNKS - 1) * size

    for j in range(2):
        cols = slice(j * cut * shard, (j + 1) * cut * shard)
        part = slice(j * cut, (j + 1) * cut)
        late[part] = dot_rows(act[:head, cols], q_recv[:head, :]).reshape(cut, shard, narrow)
    q_copy(CHUNKS - 1).wait_recv()
    for j in range(2):
        cols = slice(j * cut * shard, (j + 1) * cut * shard)
        part = slice(j * cut, (j + 1) * cut)
        late[part] += dot_rows(act[head:, cols], q_recv[head:, :]).reshape(cut, shard, narrow)
    copy = send_half(0, late, l_send, l_recv, l_sems)
    waits.append(copy)
    back_part(CHUNKS - 1)

    g_send[0] = gain_acc[...]
    for level in range(len(bits)):
        g_copy = remote(g_send.at[level], g_recv.at[level], g_sems, level, level)
        g_copy.start()
        waits.append(g_copy)
        if level < last:
            add_half(level, late, l_recv, copy)
            copy = send_half(level + 1, late, l_send, l_recv, l_sems)
            waits.append(copy)
        g_copy.wait_recv()
        total = g_send[level] + g_recv[level]
        if level < last:
            g_send[level + 1] = total
        else:
            gg_ref[...] = jnp.sum(total, axis=0, keepdims=True) * scale
    add_half(last, early, e_recv, e_last)
    gd_ref[1] = early[0, :shard, :] * scale
    gp_ref[...] = early[0, shard:, :] * scale
    copy.wait_recv()
    gd_ref[far_tap] = late[mine[last]] * scale
    gd_ref[2 - far_tap] = l_recv[n - 2].astype(F32) * scale

    for copy in waits:
        copy.wait_send()

    @pl.loop(0, CHUNKS)
    def _(c):
        p_copy(c).wait_send()
        q_copy(c).wait_send()


def paired_device(inputs, gain, w_dilated, w_point, cotangent):
    num_seqs, bins, channels = inputs.shape
    narrow = w_point.shape[0]
    n = lax.axis_size("seq")
    rows, shard = num_seqs * bins, channels // n
    levels = n.bit_length() - 1
    vmem = pl.BlockSpec(memory_space=pltpu.VMEM)
    dma = pltpu.SemaphoreType.DMA
    wide, slim = (rows, channels), (rows, narrow)
    outputs, grad_inputs, gd, gp, gg = pl.pallas_call(
        lambda *refs: block_kernel(n, *refs),
        out_shape=[
            jax.ShapeDtypeStruct(wide, BF16),
            jax.ShapeDtypeStruct(wide, BF16),
            jax.ShapeDtypeStruct((3, shard, narrow), F32),
            jax.ShapeDtypeStruct((shard, narrow), F32),
            jax.ShapeDtypeStruct((1, channels), F32),
        ],
        in_specs=[vmem] * 5,
        out_specs=[vmem] * 5,
        scratch_shapes=[
            pltpu.VMEM(wide, BF16),
            pltpu.VMEM(slim, F32),
            pltpu.VMEM(slim, BF16),
            pltpu.VMEM(slim, BF16),
            pltpu.VMEM(slim, BF16),
            pltpu.VMEM(slim, BF16),
            pltpu.VMEM(slim, BF16),
            pltpu.VMEM(wide, F32),
            pltpu.VMEM((rows, 1), F32),
            pltpu.VMEM((rows, 1), F32),
            pltpu.VMEM((n, 2 * shard, narrow), F32),
            pltpu.VMEM((n, shard, narrow), F32),
            pltpu.VMEM((8, channels), F32),
            pltpu.VMEM((n, 2 * shard, narrow), BF16),
            pltpu.VMEM((n, 2 * shard, narrow), BF16),
            pltpu.VMEM((n, shard, narrow), BF16),
            pltpu.VMEM((n, shard, narrow), BF16),
            pltpu.VMEM((levels, 8, channels), F32),
            pltpu.VMEM((levels, 8, channels), F32),
            dma((2, CHUNKS)),
            dma((2, CHUNKS)),
            dma((2, levels)),
            dma((2, levels)),
            dma((2, levels)),
        ],
        compiler_params=pltpu.CompilerParams(
            collective_id=0, has_side_effects=True, vmem_limit_bytes=56 * 1024 * 1024
        ),
    )(
        inputs.reshape(wide), gain.reshape(1, channels), w_dilated, w_point,
        cotangent.reshape(wide),
    )
    mine = lax.dynamic_slice(gg.reshape(-1), (lax.axis_index("seq") * shard,), (shard,))
    return outputs.reshape(inputs.shape), grad_inputs.reshape(inputs.shape), gd, gp.T, mine


def any_device(inputs, *rest):
    paired = lax.axis_size("seq") * inputs.shape[1] == 2 * DILATION
    return (paired_device if paired else per_device)(inputs, *rest)


def solution(mesh):
    in_specs = (P("groups", "seq", None), P(), P(), P(), P("groups", "seq", None))
    out_specs = (
        P("groups", "seq", None),
        P("groups", "seq", None),
        P("groups", "seq", None),
        P("groups", "seq"),
        P(("groups", "seq")),
    )
    return jax.shard_map(
        any_device, mesh=mesh, in_specs=in_specs, out_specs=out_specs, check_vma=False
    )
```

```python
import jax
import jax.numpy as jnp
from jax import lax
from jax.experimental import pallas as pl
from jax.experimental.pallas import tpu as pltpu
from jax.sharding import PartitionSpec as P

DILATION = 4096
F32, BF16 = jnp.float32, jnp.bfloat16


def gelu_fn(value):
    return jax.nn.gelu(value, approximate=True)


def gelu_back(value, upstream):
    return jax.vjp(gelu_fn, value)[1](upstream)[0]


def dot(a, b):
    return jnp.dot(a, b, preferred_element_type=F32)


def dot_rows(a, b):
    return lax.dot_general(a, b, (((0,), (0,)), ((), ())), preferred_element_type=F32)


def dot_last(a, b):
    return lax.dot_general(a, b, (((1,), (1,)), ((), ())), preferred_element_type=F32)


def swap(value, bit):
    n = lax.axis_size("seq")
    return lax.ppermute(value, "seq", [(s, s ^ bit) for s in range(n)])


def shifted(value, steps):
    n = lax.axis_size("seq")
    return lax.ppermute(
        value, "seq", [(s, s + steps) for s in range(max(0, -steps), min(n, n - steps))]
    )


def halves(blocks, bit):
    pairs = blocks.reshape(blocks.shape[0] // 2, 2, *blocks.shape[1:])
    mine = (lax.axis_index("seq") & bit) != 0
    keep = jnp.where(mine, pairs[:, 1], pairs[:, 0])
    send = jnp.where(mine, pairs[:, 0], pairs[:, 1])
    return keep, send.astype(BF16)


def reduced(blocks, last=True):
    n = lax.axis_size("seq")
    bit = 1
    while bit < (n if last else n // 2):
        keep, send = halves(blocks, bit)
        blocks = keep + swap(send, bit).astype(F32)
        bit *= 2
    return blocks


def per_device(inputs, gain, w_dilated, w_point, cotangent):
    num_seqs, bins, channels = inputs.shape
    narrow = w_point.shape[0]
    n = lax.axis_size("seq")
    hops = DILATION // bins
    paired = n == 2 * hops
    rows_total = num_seqs * bins * n
    scale = lax.rsqrt(F32(rows_total))
    shard = channels // n
    upper = lax.axis_index("seq") >= hops

    if paired:
        w_far = jnp.where(upper, w_dilated[2], w_dilated[0])
        w_all = jnp.concatenate([w_far, w_dilated[1]], axis=1)
    else:
        w_all = jnp.concatenate([w_dilated[0], w_dilated[2], w_dilated[1]], axis=1)

    def exchange(value):
        if paired:
            return [swap(value[0], hops)]
        return [shifted(value[0], hops), shifted(value[-1], -hops)]

    def normalize(b):
        x = inputs[b].astype(F32)
        mid = x - jnp.mean(x, axis=-1, keepdims=True)
        inv = lax.rsqrt(jnp.mean(mid * mid, axis=-1, keepdims=True) + 1e-05)
        return x, mid * inv, inv

    acts, own, sent = [], [], []
    for b in range(num_seqs):
        _, xhat, _ = normalize(b)
        act = gelu_fn(xhat * gain).astype(BF16)
        acts.append(act)
        product = dot(act, w_all)
        far = product[:, :-narrow].astype(BF16)
        own.append(product[:, -narrow:])
        sent.append(exchange([far[:, :narrow], far[:, -narrow:]]))

    outs, hids, grads_pre, arrived = [], [], [], []
    for b in range(num_seqs):
        grad_hid = dot_last(cotangent[b], w_point)
        pre = own[b]
        for term in sent[b]:
            pre = pre + term.astype(F32)
        hid = gelu_fn(pre).astype(BF16)
        grad_pre = gelu_back(pre, grad_hid).astype(BF16)
        arrived.append(exchange([grad_pre, grad_pre]))
        hids.append(hid)
        grads_pre.append(grad_pre)
        outs.append((inputs[b].astype(F32) + dot(hid, w_point)).astype(BF16))
    outputs = jnp.stack(outs)

    act_all = jnp.concatenate(acts)
    point_terms = dot_rows(cotangent.reshape(-1, channels), jnp.concatenate(hids))
    centre_terms = dot_rows(act_all, jnp.concatenate(grads_pre))
    early = jnp.concatenate(
        [centre_terms.reshape(n, shard, narrow), point_terms.reshape(n, shard, narrow)], axis=1
    )
    early = reduced(early)[0] * scale

    grad_in, gain_terms = [], jnp.zeros((channels,), F32)
    for b in range(num_seqs):
        _, xhat, inv = normalize(b)
        normed = xhat * gain
        if paired:
            back = jnp.concatenate([arrived[b][0], grads_pre[b]], axis=1)
        else:
            back = jnp.concatenate([arrived[b][1], arrived[b][0], grads_pre[b]], axis=1)
        grad_act = dot_last(back, w_all)
        grad_normed = gelu_back(normed, grad_act)
        gain_terms = gain_terms + jnp.sum(grad_normed * xhat, axis=0)
        gx = grad_normed * gain
        part = inv * (
            gx
            - jnp.mean(gx, axis=-1, keepdims=True)
            - xhat * jnp.mean(gx * xhat, axis=-1, keepdims=True)
        )
        grad_in.append((cotangent[b].astype(F32) + part).astype(BF16))
    grad_inputs = jnp.stack(grad_in)

    gain_block = jnp.pad(gain_terms.reshape(n, 1, shard), ((0, 0), (0, 15), (0, narrow - shard)))
    if paired:
        far_terms = dot_rows(act_all, jnp.concatenate([a[0] for a in arrived]))
        late = jnp.concatenate([far_terms.reshape(n, shard, narrow), gain_block], axis=1)
        late = reduced(late, last=False)
        keep, send = halves(late, n // 2)
        keep, other = keep[0], swap(send, n // 2)[0].astype(F32)
        first = jnp.where(upper, other[:shard], keep[:shard])
        final = jnp.where(upper, keep[:shard], other[:shard])
        gain_sum = keep[shard, :shard] + other[shard, :shard]
    else:
        zero_terms = dot_rows(act_all, jnp.concatenate([a[1] for a in arrived]))
        two_terms = dot_rows(act_all, jnp.concatenate([a[0] for a in arrived]))
        late = jnp.concatenate(
            [zero_terms.reshape(n, shard, narrow), two_terms.reshape(n, shard, narrow), gain_block],
            axis=1,
        )
        late = reduced(late)[0]
        first, final = late[:shard], late[shard : 2 * shard]
        gain_sum = late[2 * shard, :shard]
    grad_dilated = jnp.stack([first * scale, early[:shard], final * scale])
    return outputs, grad_inputs, grad_dilated, early[shard:].T, gain_sum * scale

CHUNKS = 4
ROOT = 0.7978845608028654


def gelu_parts(v):
    square = v * v
    t = jnp.tanh(ROOT * v * (1.0 + 0.044715 * square))
    half = 0.5 * (1.0 + t)
    slope = half + 0.5 * v * (1.0 - t * t) * (ROOT * (1.0 + 3 * 0.044715 * square))
    return v * half, slope


def block_kernel(
    n, x_ref, gain_ref, w_ref, wp_ref, cot_ref,
    out_ref, gin_ref, gd_ref, gp_ref, gg_ref,
    act, own, p_send, p_recv, q, q_recv, hid, slope, mean_s, inv_s,
    early, late, gain_acc, e_send, e_recv, l_send, l_recv, g_send, g_recv,
    p_sems, q_sems, e_sems, l_sems, g_sems,
):
    me = lax.axis_index("seq")
    rows, channels = x_ref.shape
    narrow = wp_ref.shape[0]
    shard = channels // n
    size = rows // CHUNKS
    bits, bit = [], 1
    while bit < n:
        bits.append(bit)
        bit *= 2
    mine = [(me // b) % 2 for b in bits]
    partners = [me + b * (1 - 2 * m) for b, m in zip(bits, mine)]
    upper = mine[-1]
    far_tap = 2 * upper
    scale = F32((rows * n) ** -0.5)

    barrier = pltpu.get_barrier_semaphore()
    for partner in partners:
        pl.semaphore_signal(
            barrier, inc=1, device_id={"seq": partner}, device_id_type=pl.DeviceIdType.MESH
        )

    def remote(src, dst, sems, i, level):
        return pltpu.make_async_remote_copy(
            src_ref=src, dst_ref=dst, send_sem=sems.at[0, i], recv_sem=sems.at[1, i],
            device_id={"seq": partners[level]}, device_id_type=pl.DeviceIdType.MESH,
        )

    def span(c):
        return pl.ds(pl.multiple_of(c * size, size), size)

    def p_copy(c):
        return remote(p_send.at[span(c)], p_recv.at[span(c)], p_sems, c, -1)

    def q_copy(c):
        return remote(q.at[span(c)], q_recv.at[span(c)], q_sems, c, -1)

    def first_part(c):
        r = span(c)
        x = x_ref[r, :].astype(F32)
        mean = jnp.mean(x, axis=-1, keepdims=True)
        mid = x - mean
        inv = lax.rsqrt(jnp.mean(mid * mid, axis=-1, keepdims=True) + 1e-05)
        value, grad = gelu_parts(mid * inv * gain_ref[...].reshape(1, channels))
        value = value.astype(BF16)
        p_send[r, :] = dot(value, w_ref[far_tap]).astype(BF16)
        act[r, :] = value
        slope[r, :] = grad
        mean_s[r, :] = mean
        inv_s[r, :] = inv

    first_part(0)
    pl.semaphore_wait(barrier, len(bits))
    p_copy(0).start()

    @pl.loop(1, CHUNKS)
    def _(c):
        first_part(c)
        p_copy(c).start()

    @pl.loop(0, CHUNKS)
    def _(c):
        r = span(c)
        own[r, :] = dot(act[r, :], w_ref[1])

    @pl.loop(0, CHUNKS)
    def _(c):
        r = span(c)
        grad_hid = dot_last(cot_ref[r, :], wp_ref[...])
        p_copy(c).wait_recv()
        value, grad = gelu_parts(own[r, :] + p_recv[r, :].astype(F32))
        q[r, :] = (grad * grad_hid).astype(BF16)
        q_copy(c).start()
        value = value.astype(BF16)
        hid[r, :] = value
        out_ref[r, :] = (x_ref[r, :].astype(F32) + dot(value, wp_ref[...])).astype(BF16)

    cut = n // 2
    for j in range(2):
        cols = slice(j * cut * shard, (j + 1) * cut * shard)
        part = slice(j * cut, (j + 1) * cut)
        early[part, :shard, :] = dot_rows(act[:, cols], q[...]).reshape(cut, shard, narrow)
        early[part, shard:, :] = dot_rows(cot_ref[:, cols], hid[...]).reshape(cut, shard, narrow)

    def send_half(level, cur, sends, recvs, sems):
        count = n >> (level + 1)
        base = n - 2 * count

        @pl.loop(0, count)
        def _(i):
            sends[base + i] = cur[2 * i + 1 - mine[level]].astype(BF16)

        copy = remote(
            sends.at[pl.ds(base, count)], recvs.at[pl.ds(base, count)], sems, level, level
        )
        copy.start()
        return copy

    def add_half(level, cur, recvs, copy):
        count = n >> (level + 1)
        base = n - 2 * count
        copy.wait_recv()

        @pl.loop(0, count)
        def _(i):
            cur[i] = cur[2 * i + mine[level]] + recvs[base + i].astype(F32)

    waits = []
    last = len(bits) - 1

    def back_part(c):
        r = span(c)
        grad_act = dot_last(q[r, :], w_ref[1]) + dot_last(q_recv[r, :], w_ref[far_tap])
        inv = inv_s[r, :]
        xhat = (x_ref[r, :].astype(F32) - mean_s[r, :]) * inv
        gn = grad_act * slope[r, :]
        gain_acc[...] += jnp.sum((gn * xhat).reshape(size // 8, 8, channels), axis=0)
        gx = gn * gain_ref[...].reshape(1, channels)
        m1 = jnp.mean(gx, axis=-1, keepdims=True)
        m2 = jnp.mean(gx * xhat, axis=-1, keepdims=True)
        gin_ref[r, :] = (cot_ref[r, :].astype(F32) + inv * (gx - m1 - xhat * m2)).astype(BF16)

    gain_acc[...] = jnp.zeros_like(gain_acc)
    for level in range(last):
        copy = send_half(level, early, e_send, e_recv, e_sems)
        waits.append(copy)
        q_copy(level).wait_recv()
        back_part(level)
        add_half(level, early, e_recv, copy)
    e_last = send_half(last, early, e_send, e_recv, e_sems)
    waits.append(e_last)
    head = (CHUNKS - 1) * size

    @pl.loop(last, CHUNKS - 1)
    def _(c):
        q_copy(c).wait_recv()
        back_part(c)

    for j in range(2):
        cols = slice(j * cut * shard, (j + 1) * cut * shard)
        part = slice(j * cut, (j + 1) * cut)
        late[part] = dot_rows(act[:head, cols], q_recv[:head, :]).reshape(cut, shard, narrow)
    q_copy(CHUNKS - 1).wait_recv()
    for j in range(2):
        cols = slice(j * cut * shard, (j + 1) * cut * shard)
        part = slice(j * cut, (j + 1) * cut)
        late[part] += dot_rows(act[head:, cols], q_recv[head:, :]).reshape(cut, shard, narrow)
    copy = send_half(0, late, l_send, l_recv, l_sems)
    waits.append(copy)
    back_part(CHUNKS - 1)

    g_send[0] = gain_acc[...]
    for level in range(len(bits)):
        g_copy = remote(g_send.at[level], g_recv.at[level], g_sems, level, level)
        g_copy.start()
        waits.append(g_copy)
        if level < last:
            add_half(level, late, l_recv, copy)
            copy = send_half(level + 1, late, l_send, l_recv, l_sems)
            waits.append(copy)
        g_copy.wait_recv()
        total = g_send[level] + g_recv[level]
        if level < last:
            g_send[level + 1] = total
        else:
            total = jnp.sum(total, axis=0, keepdims=True) * scale
            picked = total[:, :shard]
            for s in range(1, n):
                picked = jnp.where(me == s, total[:, s * shard : (s + 1) * shard], picked)
            gg_ref[...] = picked
    add_half(last, early, e_recv, e_last)
    gd_ref[1] = early[0, :shard, :] * scale
    gp_ref[...] = early[0, shard:, :] * scale
    copy.wait_recv()
    gd_ref[far_tap] = late[mine[last]] * scale
    gd_ref[2 - far_tap] = l_recv[n - 2].astype(F32) * scale

    for copy in waits:
        copy.wait_send()

    @pl.loop(0, CHUNKS)
    def _(c):
        p_copy(c).wait_send()
        q_copy(c).wait_send()


def paired_device(inputs, gain, w_dilated, w_point, cotangent):
    num_seqs, bins, channels = inputs.shape
    narrow = w_point.shape[0]
    n = lax.axis_size("seq")
    rows, shard = num_seqs * bins, channels // n
    levels = n.bit_length() - 1
    vmem = pl.BlockSpec(memory_space=pltpu.VMEM)
    dma = pltpu.SemaphoreType.DMA
    wide, slim = (rows, channels), (rows, narrow)
    outputs, grad_inputs, gd, gp, gg = pl.pallas_call(
        lambda *refs: block_kernel(n, *refs),
        out_shape=[
            jax.ShapeDtypeStruct(wide, BF16),
            jax.ShapeDtypeStruct(wide, BF16),
            jax.ShapeDtypeStruct((3, shard, narrow), F32),
            jax.ShapeDtypeStruct((shard, narrow), F32),
            jax.ShapeDtypeStruct((1, shard), F32),
        ],
        in_specs=[vmem] * 5,
        out_specs=[vmem] * 5,
        scratch_shapes=[
            pltpu.VMEM(wide, BF16),
            pltpu.VMEM(slim, F32),
            pltpu.VMEM(slim, BF16),
            pltpu.VMEM(slim, BF16),
            pltpu.VMEM(slim, BF16),
            pltpu.VMEM(slim, BF16),
            pltpu.VMEM(slim, BF16),
            pltpu.VMEM(wide, F32),
            pltpu.VMEM((rows, 1), F32),
            pltpu.VMEM((rows, 1), F32),
            pltpu.VMEM((n, 2 * shard, narrow), F32),
            pltpu.VMEM((n, shard, narrow), F32),
            pltpu.VMEM((8, channels), F32),
            pltpu.VMEM((n, 2 * shard, narrow), BF16),
            pltpu.VMEM((n, 2 * shard, narrow), BF16),
            pltpu.VMEM((n, shard, narrow), BF16),
            pltpu.VMEM((n, shard, narrow), BF16),
            pltpu.VMEM((levels, 8, channels), F32),
            pltpu.VMEM((levels, 8, channels), F32),
            dma((2, CHUNKS)),
            dma((2, CHUNKS)),
            dma((2, levels)),
            dma((2, levels)),
            dma((2, levels)),
        ],
        compiler_params=pltpu.CompilerParams(
            collective_id=0, has_side_effects=True, vmem_limit_bytes=56 * 1024 * 1024
        ),
    )(
        inputs.reshape(wide), gain, w_dilated, w_point,
        cotangent.reshape(wide),
    )
    step = rows // 2
    tall = pl.BlockSpec((step, channels), lambda i: (i, 0))
    taps = pl.BlockSpec(gd.shape, lambda i: (0, 0, 0))
    gains = pl.BlockSpec(gg.shape, lambda i: (0, 0))
    outputs, grad_inputs, gd, gg = pl.pallas_call(
        deliver,
        grid=(2,),
        out_shape=[jax.ShapeDtypeStruct(a.shape, a.dtype) for a in (outputs, grad_inputs, gd, gg)],
        in_specs=[tall, tall, taps, gains],
        out_specs=[tall, tall, taps, gains],
    )(outputs, grad_inputs, gd, gg)
    return (
        outputs.reshape(inputs.shape), grad_inputs.reshape(inputs.shape), gd, gp.T, gg.reshape(-1)
    )


def deliver(*refs):
    for source, target in zip(refs[:4], refs[4:]):
        target[...] = source[...]


def any_device(inputs, *rest):
    paired = lax.axis_size("seq") * inputs.shape[1] == 2 * DILATION
    return (paired_device if paired else per_device)(inputs, *rest)


def solution(mesh):
    in_specs = (P("groups", "seq", None), P(), P(), P(), P("groups", "seq", None))
    out_specs = (
        P("groups", "seq", None),
        P("groups", "seq", None),
        P("groups", "seq", None),
        P("groups", "seq"),
        P(("groups", "seq")),
    )
    return jax.shard_map(
        any_device, mesh=mesh, in_specs=in_specs, out_specs=out_specs, check_vma=False
    )
```

```python
import jax
import jax.numpy as jnp
from jax import lax
from jax.experimental import pallas as pl
from jax.experimental.pallas import tpu as pltpu
from jax.sharding import PartitionSpec as P

DILATION = 4096
F32, BF16 = jnp.float32, jnp.bfloat16


def gelu_fn(value):
    return jax.nn.gelu(value, approximate=True)


def gelu_back(value, upstream):
    return jax.vjp(gelu_fn, value)[1](upstream)[0]


def dot(a, b):
    return jnp.dot(a, b, preferred_element_type=F32)


def dot_rows(a, b):
    return lax.dot_general(a, b, (((0,), (0,)), ((), ())), preferred_element_type=F32)


def dot_last(a, b):
    return lax.dot_general(a, b, (((1,), (1,)), ((), ())), preferred_element_type=F32)


def swap(value, bit):
    n = lax.axis_size("seq")
    return lax.ppermute(value, "seq", [(s, s ^ bit) for s in range(n)])


def shifted(value, steps):
    n = lax.axis_size("seq")
    return lax.ppermute(
        value, "seq", [(s, s + steps) for s in range(max(0, -steps), min(n, n - steps))]
    )


def halves(blocks, bit):
    pairs = blocks.reshape(blocks.shape[0] // 2, 2, *blocks.shape[1:])
    mine = (lax.axis_index("seq") & bit) != 0
    keep = jnp.where(mine, pairs[:, 1], pairs[:, 0])
    send = jnp.where(mine, pairs[:, 0], pairs[:, 1])
    return keep, send.astype(BF16)


def reduced(blocks, last=True):
    n = lax.axis_size("seq")
    bit = 1
    while bit < (n if last else n // 2):
        keep, send = halves(blocks, bit)
        blocks = keep + swap(send, bit).astype(F32)
        bit *= 2
    return blocks


def per_device(inputs, gain, w_dilated, w_point, cotangent):
    num_seqs, bins, channels = inputs.shape
    narrow = w_point.shape[0]
    n = lax.axis_size("seq")
    hops = DILATION // bins
    paired = n == 2 * hops
    rows_total = num_seqs * bins * n
    scale = lax.rsqrt(F32(rows_total))
    shard = channels // n
    upper = lax.axis_index("seq") >= hops

    if paired:
        w_far = jnp.where(upper, w_dilated[2], w_dilated[0])
        w_all = jnp.concatenate([w_far, w_dilated[1]], axis=1)
    else:
        w_all = jnp.concatenate([w_dilated[0], w_dilated[2], w_dilated[1]], axis=1)

    def exchange(value):
        if paired:
            return [swap(value[0], hops)]
        return [shifted(value[0], hops), shifted(value[-1], -hops)]

    def normalize(b):
        x = inputs[b].astype(F32)
        mid = x - jnp.mean(x, axis=-1, keepdims=True)
        inv = lax.rsqrt(jnp.mean(mid * mid, axis=-1, keepdims=True) + 1e-05)
        return x, mid * inv, inv

    acts, own, sent = [], [], []
    for b in range(num_seqs):
        _, xhat, _ = normalize(b)
        act = gelu_fn(xhat * gain).astype(BF16)
        acts.append(act)
        product = dot(act, w_all)
        far = product[:, :-narrow].astype(BF16)
        own.append(product[:, -narrow:])
        sent.append(exchange([far[:, :narrow], far[:, -narrow:]]))

    outs, hids, grads_pre, arrived = [], [], [], []
    for b in range(num_seqs):
        grad_hid = dot_last(cotangent[b], w_point)
        pre = own[b]
        for term in sent[b]:
            pre = pre + term.astype(F32)
        hid = gelu_fn(pre).astype(BF16)
        grad_pre = gelu_back(pre, grad_hid).astype(BF16)
        arrived.append(exchange([grad_pre, grad_pre]))
        hids.append(hid)
        grads_pre.append(grad_pre)
        outs.append((inputs[b].astype(F32) + dot(hid, w_point)).astype(BF16))
    outputs = jnp.stack(outs)

    act_all = jnp.concatenate(acts)
    point_terms = dot_rows(cotangent.reshape(-1, channels), jnp.concatenate(hids))
    centre_terms = dot_rows(act_all, jnp.concatenate(grads_pre))
    early = jnp.concatenate(
        [centre_terms.reshape(n, shard, narrow), point_terms.reshape(n, shard, narrow)], axis=1
    )
    early = reduced(early)[0] * scale

    grad_in, gain_terms = [], jnp.zeros((channels,), F32)
    for b in range(num_seqs):
        _, xhat, inv = normalize(b)
        normed = xhat * gain
        if paired:
            back = jnp.concatenate([arrived[b][0], grads_pre[b]], axis=1)
        else:
            back = jnp.concatenate([arrived[b][1], arrived[b][0], grads_pre[b]], axis=1)
        grad_act = dot_last(back, w_all)
        grad_normed = gelu_back(normed, grad_act)
        gain_terms = gain_terms + jnp.sum(grad_normed * xhat, axis=0)
        gx = grad_normed * gain
        part = inv * (
            gx
            - jnp.mean(gx, axis=-1, keepdims=True)
            - xhat * jnp.mean(gx * xhat, axis=-1, keepdims=True)
        )
        grad_in.append((cotangent[b].astype(F32) + part).astype(BF16))
    grad_inputs = jnp.stack(grad_in)

    gain_block = jnp.pad(gain_terms.reshape(n, 1, shard), ((0, 0), (0, 15), (0, narrow - shard)))
    if paired:
        far_terms = dot_rows(act_all, jnp.concatenate([a[0] for a in arrived]))
        late = jnp.concatenate([far_terms.reshape(n, shard, narrow), gain_block], axis=1)
        late = reduced(late, last=False)
        keep, send = halves(late, n // 2)
        keep, other = keep[0], swap(send, n // 2)[0].astype(F32)
        first = jnp.where(upper, other[:shard], keep[:shard])
        final = jnp.where(upper, keep[:shard], other[:shard])
        gain_sum = keep[shard, :shard] + other[shard, :shard]
    else:
        zero_terms = dot_rows(act_all, jnp.concatenate([a[1] for a in arrived]))
        two_terms = dot_rows(act_all, jnp.concatenate([a[0] for a in arrived]))
        late = jnp.concatenate(
            [zero_terms.reshape(n, shard, narrow), two_terms.reshape(n, shard, narrow), gain_block],
            axis=1,
        )
        late = reduced(late)[0]
        first, final = late[:shard], late[shard : 2 * shard]
        gain_sum = late[2 * shard, :shard]
    grad_dilated = jnp.stack([first * scale, early[:shard], final * scale])
    return outputs, grad_inputs, grad_dilated, early[shard:].T, gain_sum * scale

CHUNKS = 4
ROOT = 0.7978845608028654


def gelu_parts(v):
    square = v * v
    t = jnp.tanh(ROOT * v * (1.0 + 0.044715 * square))
    half = 0.5 * (1.0 + t)
    slope = half + 0.5 * v * (1.0 - t * t) * (ROOT * (1.0 + 3 * 0.044715 * square))
    return v * half, slope


def block_kernel(
    n, x_ref, gain_ref, w_ref, wp_ref, cot_ref,
    out_ref, gin_ref, gd_ref, gp_ref, gg_ref,
    act, own, p_send, p_recv, q, q_recv, hid, slope, mean_s, inv_s,
    early, late, gain_acc, e_send, e_recv, l_send, l_recv, g_send, g_recv,
    p_sems, q_sems, e_sems, l_sems, g_sems,
):
    me = lax.axis_index("seq")
    rows, channels = x_ref.shape
    narrow = wp_ref.shape[0]
    shard = channels // n
    size = rows // CHUNKS
    bits, bit = [], 1
    while bit < n:
        bits.append(bit)
        bit *= 2
    mine = [(me // b) % 2 for b in bits]
    partners = [me + b * (1 - 2 * m) for b, m in zip(bits, mine)]
    upper = mine[-1]
    far_tap = 2 * upper
    scale = F32((rows * n) ** -0.5)

    barrier = pltpu.get_barrier_semaphore()
    for partner in partners:
        pl.semaphore_signal(
            barrier, inc=1, device_id={"seq": partner}, device_id_type=pl.DeviceIdType.MESH
        )

    def remote(src, dst, sems, i, level):
        return pltpu.make_async_remote_copy(
            src_ref=src, dst_ref=dst, send_sem=sems.at[0, i], recv_sem=sems.at[1, i],
            device_id={"seq": partners[level]}, device_id_type=pl.DeviceIdType.MESH,
        )

    def span(c):
        return pl.ds(pl.multiple_of(c * size, size), size)

    def p_copy(c):
        return remote(p_send.at[span(c)], p_recv.at[span(c)], p_sems, c, -1)

    def q_copy(c):
        return remote(q.at[span(c)], q_recv.at[span(c)], q_sems, c, -1)

    def first_part(c):
        r = span(c)
        x = x_ref[r, :].astype(F32)
        mean = jnp.mean(x, axis=-1, keepdims=True)
        mid = x - mean
        inv = lax.rsqrt(jnp.mean(mid * mid, axis=-1, keepdims=True) + 1e-05)
        value, grad = gelu_parts(mid * inv * gain_ref[...].reshape(1, channels))
        value = value.astype(BF16)
        p_send[r, :] = dot(value, w_ref[far_tap]).astype(BF16)
        act[r, :] = value
        slope[r, :] = grad
        mean_s[r, :] = mean
        inv_s[r, :] = inv

    first_part(0)
    pl.semaphore_wait(barrier, len(bits))
    p_copy(0).start()

    @pl.loop(1, CHUNKS)
    def _(c):
        first_part(c)
        p_copy(c).start()

    @pl.loop(0, CHUNKS)
    def _(c):
        r = span(c)
        own[r, :] = dot(act[r, :], w_ref[1])

    @pl.loop(0, CHUNKS)
    def _(c):
        r = span(c)
        grad_hid = dot_last(cot_ref[r, :], wp_ref[...])
        p_copy(c).wait_recv()
        value, grad = gelu_parts(own[r, :] + p_recv[r, :].astype(F32))
        q[r, :] = (grad * grad_hid).astype(BF16)
        q_copy(c).start()
        value = value.astype(BF16)
        hid[r, :] = value
        out_ref[r, :] = (x_ref[r, :].astype(F32) + dot(value, wp_ref[...])).astype(BF16)

    cut = n // 2
    for j in range(2):
        cols = slice(j * cut * shard, (j + 1) * cut * shard)
        part = slice(j * cut, (j + 1) * cut)
        early[part, :shard, :] = dot_rows(act[:, cols], q[...]).reshape(cut, shard, narrow)
        early[part, shard:, :] = dot_rows(cot_ref[:, cols], hid[...]).reshape(cut, shard, narrow)

    def send_half(level, cur, sends, recvs, sems):
        count = n >> (level + 1)
        base = n - 2 * count

        @pl.loop(0, count)
        def _(i):
            sends[base + i] = cur[2 * i + 1 - mine[level]].astype(BF16)

        copy = remote(
            sends.at[pl.ds(base, count)], recvs.at[pl.ds(base, count)], sems, level, level
        )
        copy.start()
        return copy

    def add_half(level, cur, recvs, copy):
        count = n >> (level + 1)
        base = n - 2 * count
        copy.wait_recv()

        @pl.loop(0, count)
        def _(i):
            cur[i] = cur[2 * i + mine[level]] + recvs[base + i].astype(F32)

    waits = []
    last = len(bits) - 1

    def back_part(c):
        r = span(c)
        grad_act = dot_last(q[r, :], w_ref[1]) + dot_last(q_recv[r, :], w_ref[far_tap])
        inv = inv_s[r, :]
        xhat = (x_ref[r, :].astype(F32) - mean_s[r, :]) * inv
        gn = grad_act * slope[r, :]
        gain_acc[...] += jnp.sum((gn * xhat).reshape(size // 8, 8, channels), axis=0)
        gx = gn * gain_ref[...].reshape(1, channels)
        m1 = jnp.mean(gx, axis=-1, keepdims=True)
        m2 = jnp.mean(gx * xhat, axis=-1, keepdims=True)
        gin_ref[r, :] = (cot_ref[r, :].astype(F32) + inv * (gx - m1 - xhat * m2)).astype(BF16)

    gain_acc[...] = jnp.zeros_like(gain_acc)
    for level in range(last):
        copy = send_half(level, early, e_send, e_recv, e_sems)
        waits.append(copy)
        q_copy(level).wait_recv()
        back_part(level)
        add_half(level, early, e_recv, copy)
    e_last = send_half(last, early, e_send, e_recv, e_sems)
    waits.append(e_last)
    head = (CHUNKS - 1) * size

    @pl.loop(last, CHUNKS - 1)
    def _(c):
        q_copy(c).wait_recv()
        back_part(c)

    for j in range(2):
        cols = slice(j * cut * shard, (j + 1) * cut * shard)
        part = slice(j * cut, (j + 1) * cut)
        late[part] = dot_rows(act[:head, cols], q_recv[:head, :]).reshape(cut, shard, narrow)
    q_copy(CHUNKS - 1).wait_recv()
    for j in range(2):
        cols = slice(j * cut * shard, (j + 1) * cut * shard)
        part = slice(j * cut, (j + 1) * cut)
        late[part] += dot_rows(act[head:, cols], q_recv[head:, :]).reshape(cut, shard, narrow)
    copy = send_half(0, late, l_send, l_recv, l_sems)
    waits.append(copy)
    back_part(CHUNKS - 1)

    g_send[0] = gain_acc[...]
    for level in range(len(bits)):
        g_copy = remote(g_send.at[level], g_recv.at[level], g_sems, level, level)
        g_copy.start()
        waits.append(g_copy)
        if level < last:
            add_half(level, late, l_recv, copy)
            copy = send_half(level + 1, late, l_send, l_recv, l_sems)
            waits.append(copy)
        if level == 0:
            add_half(last, early, e_recv, e_last)
            gd_ref[1] = early[0, :shard, :] * scale
            gp_ref[...] = early[0, shard:, :] * scale
        g_copy.wait_recv()
        total = g_send[level] + g_recv[level]
        if level < last:
            g_send[level + 1] = total
        else:
            total = jnp.sum(total, axis=0, keepdims=True) * scale
            picked = total[:, :shard]
            for s in range(1, n):
                picked = jnp.where(me == s, total[:, s * shard : (s + 1) * shard], picked)
            gg_ref[...] = picked
    copy.wait_recv()
    gd_ref[far_tap] = late[mine[last]] * scale
    gd_ref[2 - far_tap] = l_recv[n - 2].astype(F32) * scale

    for copy in waits:
        copy.wait_send()

    @pl.loop(0, CHUNKS)
    def _(c):
        p_copy(c).wait_send()
        q_copy(c).wait_send()


def paired_device(inputs, gain, w_dilated, w_point, cotangent):
    num_seqs, bins, channels = inputs.shape
    narrow = w_point.shape[0]
    n = lax.axis_size("seq")
    rows, shard = num_seqs * bins, channels // n
    levels = n.bit_length() - 1
    vmem = pl.BlockSpec(memory_space=pltpu.VMEM)
    dma = pltpu.SemaphoreType.DMA
    wide, slim = (rows, channels), (rows, narrow)
    outputs, grad_inputs, gd, gp, gg = pl.pallas_call(
        lambda *refs: block_kernel(n, *refs),
        out_shape=[
            jax.ShapeDtypeStruct(wide, BF16),
            jax.ShapeDtypeStruct(wide, BF16),
            jax.ShapeDtypeStruct((3, shard, narrow), F32),
            jax.ShapeDtypeStruct((shard, narrow), F32),
            jax.ShapeDtypeStruct((1, shard), F32),
        ],
        in_specs=[vmem] * 5,
        out_specs=[vmem] * 5,
        scratch_shapes=[
            pltpu.VMEM(wide, BF16),
            pltpu.VMEM(slim, F32),
            pltpu.VMEM(slim, BF16),
            pltpu.VMEM(slim, BF16),
            pltpu.VMEM(slim, BF16),
            pltpu.VMEM(slim, BF16),
            pltpu.VMEM(slim, BF16),
            pltpu.VMEM(wide, F32),
            pltpu.VMEM((rows, 1), F32),
            pltpu.VMEM((rows, 1), F32),
            pltpu.VMEM((n, 2 * shard, narrow), F32),
            pltpu.VMEM((n, shard, narrow), F32),
            pltpu.VMEM((8, channels), F32),
            pltpu.VMEM((n, 2 * shard, narrow), BF16),
            pltpu.VMEM((n, 2 * shard, narrow), BF16),
            pltpu.VMEM((n, shard, narrow), BF16),
            pltpu.VMEM((n, shard, narrow), BF16),
            pltpu.VMEM((levels, 8, channels), F32),
            pltpu.VMEM((levels, 8, channels), F32),
            dma((2, CHUNKS)),
            dma((2, CHUNKS)),
            dma((2, levels)),
            dma((2, levels)),
            dma((2, levels)),
        ],
        compiler_params=pltpu.CompilerParams(
            collective_id=0, has_side_effects=True, vmem_limit_bytes=56 * 1024 * 1024
        ),
    )(
        inputs.reshape(wide), gain, w_dilated, w_point,
        cotangent.reshape(wide),
    )
    step = rows // 2
    tall = pl.BlockSpec((step, channels), lambda i: (i, 0))
    taps = pl.BlockSpec(gd.shape, lambda i: (0, 0, 0))
    gains = pl.BlockSpec(gg.shape, lambda i: (0, 0))
    outputs, grad_inputs, gd, gg = pl.pallas_call(
        deliver,
        grid=(2,),
        out_shape=[jax.ShapeDtypeStruct(a.shape, a.dtype) for a in (outputs, grad_inputs, gd, gg)],
        in_specs=[tall, tall, taps, gains],
        out_specs=[tall, tall, taps, gains],
    )(outputs, grad_inputs, gd, gg)
    return (
        outputs.reshape(inputs.shape), grad_inputs.reshape(inputs.shape), gd, gp.T, gg.reshape(-1)
    )


def deliver(*refs):
    for source, target in zip(refs[:4], refs[4:]):
        target[...] = source[...]


def any_device(inputs, *rest):
    paired = lax.axis_size("seq") * inputs.shape[1] == 2 * DILATION
    return (paired_device if paired else per_device)(inputs, *rest)


def solution(mesh):
    in_specs = (P("groups", "seq", None), P(), P(), P(), P("groups", "seq", None))
    out_specs = (
        P("groups", "seq", None),
        P("groups", "seq", None),
        P("groups", "seq", None),
        P("groups", "seq"),
        P(("groups", "seq")),
    )
    return jax.shard_map(
        any_device, mesh=mesh, in_specs=in_specs, out_specs=out_specs, check_vma=False
    )
```
